32 devices in a mesh: groups: 2 (over y), ao: 8 (over z, core), aux: 2 (over x).
Axes of the slice: x: 2, y: 2, z: 4, core: 2. Of those that a mesh axis runs over, the one named last changes fastest.
Arguments:
- three_index: bfloat16 [64, 32, 128, 128], P(('groups', 'ao'), 'aux'), parts along dimension 0, may hold values from -0.25 to 0.25
- orbitals: bfloat16 [1024, 512], P('ao', 'groups'), parts along dimension 1, may hold values from -0.59765625 to 0.59765625
- partners: int32 [16, 4], P(('groups', 'ao')), parts along dimension 0, may hold values from 0 to 7, all different within a row
Outputs:
- exchange: float32 [64, 128, 128], P(('groups', 'ao'), 'aux'), parts along dimension 0
The draws below stay inside these ranges and needn't reach their ends.
There are 2 independent parts, one for each index of `groups`. The reference program is written for one: setup_inputs(seed, part) draws one part's arguments, and reference() takes and returns one part's arrays. A program takes and returns all parts, laid end to end along the dimension named above; each array names one. Nothing has to cross between parts.
Inputs may be any that keep to these rules, and one draw needn't show every extreme that they name: `partners`: each row names 4 different blocks, and every block is named by some row.
All inputs are finite; a program needn't handle non-finite values.
Results may differ from the reference program's by a relative error of at most 0.0044.
Values may be sent and summed in bfloat16 or wider, within the bound.
A program may use at most 128 MiB of HBM per device.

```python
import jax
import jax.numpy as jnp
from jax import lax

BLOCK = 128
NOCC = 256
NPAIR = 4
NBLK = 8
NAO = 1024
AUX = 32
PAIRS = 32


def level_of(key, shape, cuts, low, high):
    factor_of = 1.0
    for position, blocks in cuts:
        heights = jax.random.uniform(jax.random.fold_in(jax.random.fold_in(key, 6), position), (blocks,), jnp.float32, low / len(cuts), high / len(cuts))
        factor_of = factor_of * jnp.repeat(jnp.exp(heights), shape[position] // blocks).reshape((-1,) + (1,) * (len(shape) - 1 - position))
    return factor_of


def distinct(own_key, rows, number_of, top, lift):
    sequence = jax.random.permutation(jax.random.fold_in(own_key, 1), number_of)
    pull = sequence
    for power in range(3):
        pull = pull * pull // number_of
    pull = pull * lift // number_of
    lots = jax.random.randint(jax.random.fold_in(own_key, 2), (rows, number_of), 0, 4096) + pull
    sure = jax.random.permutation(jax.random.fold_in(own_key, 3), rows)[jnp.arange(number_of) % rows]
    lots = jnp.where(jnp.arange(rows)[:, None] == sure[None, :], 1 << 14, lots)
    priority = lots * number_of + jnp.arange(number_of)
    return lax.top_k(priority.astype(jnp.int32), top)[1].astype(jnp.int32)


def gaussian(rng, extent, deviation, limit, split=(), held_as=jnp.bfloat16):
    level = level_of(rng, extent, split, -0.22, 0.18) if split else 1.0
    array = jax.random.normal(rng, extent, jnp.float32) * deviation * level
    return jnp.minimum(jnp.maximum(array, -limit), limit).astype(held_as)


def setup_inputs(seed: int = 0, part: int = 0) -> dict:
    seeds = jax.random.split(jax.random.key(seed), 4)
    own_keys = jax.random.split(jax.random.fold_in(seeds[3], part), 4)
    return {
        "three_index": gaussian(own_keys[0], (PAIRS, AUX, BLOCK, BLOCK), (NPAIR * BLOCK) ** -0.5, 0.25, ((0, 8), (1, 2))),
        "orbitals": gaussian(own_keys[1], (NAO, NOCC), 0.1, 0.59765625, ((0, 8),)),
        "partners": distinct(own_keys[2], NBLK, NBLK, NPAIR, 8192),
    }


def reference(three_index, orbitals, partners):
    coef_blocks = orbitals.reshape(NBLK, BLOCK, NOCC)
    blocks = three_index.reshape(NBLK, NPAIR, AUX, BLOCK, BLOCK)

    def half_one(args):
        block_b, row = args
        chosen = coef_blocks[row.astype(jnp.int32)]
        value = jnp.einsum("pxab,pbi->xai", block_b.astype(jnp.float32), chosen.astype(jnp.float32))
        return value.astype(jnp.bfloat16)

    half = lax.map(half_one, (blocks, partners))

    def exch_one(args):
        own, row = args
        others = half[row.astype(jnp.int32)]
        return jnp.einsum("xai,pxci->pac", own.astype(jnp.float32), others.astype(jnp.float32))

    result = lax.map(exch_one, (half, partners))
    return result.reshape(PAIRS, BLOCK, BLOCK)
```

```python
import functools

import jax
import jax.numpy as jnp
from jax import lax
from jax.experimental import pallas as pl
from jax.experimental.pallas import tpu as pltpu
from jax.sharding import PartitionSpec as P

MESH = pl.DeviceIdType.MESH


def body(
    nao, nx,
    b_hbm, c_hbm, part, out,
    b_v, c_all, csel, pall, psm, hs, hbuf, kf, sx, rx, ks, kr, own,
    b_sem, c_loc, c_send, c_fwd, c_recv, p_send, p_recv, p_loc,
    h_send, h_recv, f_send, f_recv, x_send, x_recv, k_send, k_recv,
):
    me = lax.axis_index("ao")
    x = lax.axis_index("aux")
    nz = nao // 2
    z, c = me // 2, me % 2
    sib = z * 2 + 1 - c
    npair, npl, blk, _ = b_hbm.shape
    npz = npl // nz
    ra = blk // nx
    wide = c_hbm.shape[1]
    hw = wide // 2

    def remote(src, dst, send, recv, where):
        return pltpu.make_async_remote_copy(
            src_ref=src, dst_ref=dst, send_sem=send, recv_sem=recv,
            device_id=where, device_id_type=MESH,
        )

    loads = [pltpu.make_async_copy(b_hbm.at[p], b_v.at[p], b_sem.at[p]) for p in range(npair)]
    mine = pltpu.make_async_copy(c_hbm, c_all.at[me], c_loc)
    mine.start()
    for load in loads:
        load.start()

    barrier = pltpu.get_barrier_semaphore()
    for k in range(1, nao):
        pl.semaphore_signal(barrier, inc=1, device_id={"ao": (me + k) % nao}, device_id_type=MESH)
    for k in range(1, nx):
        pl.semaphore_signal(barrier, inc=1, device_id={"aux": (x + k) % nx}, device_id_type=MESH)
    pl.semaphore_wait(barrier, nao - 1 + nx - 1)

    far = [(z + nz // 2 + k) % nz for k in range(nz)]
    here = nz - nz // 2
    others = [k for k in range(nz) if k != here]
    sent = []
    for k in others:
        copy = remote(c_hbm, c_all.at[me], c_send.at[k], c_recv.at[me], {"ao": far[k] * 2 + c})
        copy.start()
        sent.append(copy)
    copy = remote(c_hbm, c_all.at[me], c_send.at[here], c_recv.at[me], {"ao": sib})
    copy.start()
    sent.append(copy)

    lane = lax.broadcasted_iota(jnp.int32, (8, 128), 1)
    row = jnp.zeros((8, 128), jnp.int32)
    for p in range(npair):
        row = jnp.where(lane == p, part[0, p], row)
    myrow = pall.at[pl.ds(pl.multiple_of(me * 8, 8), 8)]
    myrow[...] = row
    for k in range(1, nao):
        copy = remote(myrow, myrow, p_send.at[k], p_recv.at[me], {"ao": (me + k) % nao})
        copy.start()
        sent.append(copy)

    def arrived(ref, sem):
        remote(ref, ref, sem, sem, {"ao": sib}).wait_recv()

    for k in others[::-1]:
        n = far[k] * 2 + c
        arrived(c_all.at[n], c_recv.at[n])
        copy = remote(c_all.at[n], c_all.at[n], c_fwd.at[k], c_recv.at[n], {"ao": sib})
        copy.start()
        sent.append(copy)
    for k in range(nz):
        n = far[k] * 2 + 1 - c
        arrived(c_all.at[n], c_recv.at[n])
    mine.wait()
    for load in loads:
        load.wait()
    for p in range(npair):
        csel[p * blk:(p + 1) * blk, :] = c_all[part[0, p]]

    for j in range(npz):
        for k in range(nz):
            q = far[k] * npz + j
            left = jnp.concatenate([b_v[p, q] for p in range(npair)], axis=1)
            half = jnp.dot(left, csel[...], preferred_element_type=jnp.float32).astype(jnp.bfloat16)
            hs[q, 0] = half[:, :hw]
            hs[q, 1] = half[:, hw:]
            if k == here:
                hbuf[x, j, me] = hs[q, c]
                copy = remote(hs.at[q, 1 - c], hbuf.at[x, j, me], h_send.at[q, 0], h_recv.at[j, me], {"ao": sib})
                copy.start()
                sent.append(copy)
                for d in range(1, nx):
                    copy = remote(
                        hbuf.at[x, j, me], hbuf.at[x, j, me], f_send.at[d, j, me], f_recv.at[x, j, me],
                        {"aux": (x + d) % nx},
                    )
                    copy.start()
            else:
                for cc in range(2):
                    copy = remote(
                        hs.at[q, cc], hbuf.at[x, j, me], h_send.at[q, cc], h_recv.at[j, me],
                        {"ao": far[k] * 2 + cc},
                    )
                    copy.start()
                    sent.append(copy)

    for k in range(1, nao):
        n = (me + k) % nao
        theirs = pall.at[pl.ds(pl.multiple_of(n * 8, 8), 8)]
        arrived(theirs, p_recv.at[n])
    to_smem = pltpu.make_async_copy(pall, psm, p_loc)
    to_smem.start()
    to_smem.wait()

    def add_up(xs, j, first):
        lhs = hbuf[xs, j, :, pl.ds(pl.multiple_of(x * ra, ra), ra), :].reshape(nao * ra, hw)

        def step(t, _):
            rhs = hbuf[xs, j, pl.ds(2 * t, 2)].reshape(2 * blk, hw)
            got = lax.dot_general(lhs, rhs, (((1,), (1,)), ((), ())), preferred_element_type=jnp.float32)
            if first:
                kf[2 * t] = got[:, :blk]
                kf[2 * t + 1] = got[:, blk:]
            else:
                kf[2 * t] += got[:, :blk]
                kf[2 * t + 1] += got[:, blk:]
            return 0

        lax.fori_loop(0, nao // 2, step, 0)

    def take_others(j):
        for d in range(1, nx):
            xs = (x + d) % nx

            def get(n, _):
                arrived(hbuf.at[xs, j, n], f_recv.at[xs, j, n])
                return 0

            lax.fori_loop(0, nao, get, 0)
            add_up(xs, j, False)

    for j in range(npz):
        def pass_on(t, _):
            n = (me + 1 + t) % nao
            arrived(hbuf.at[x, j, n], h_recv.at[j, n])
            for d in range(1, nx):
                remote(
                    hbuf.at[x, j, n], hbuf.at[x, j, n], f_send.at[d, j, n], f_recv.at[x, j, n],
                    {"aux": (x + d) % nx},
                ).start()
            return 0

        lax.fori_loop(0, nao - 1, pass_on, 0)
        add_up(x, j, j == 0)
        if j > 0:
            take_others(j - 1)
    take_others(npz - 1)

    def picked(m, p):
        return kf[psm[m * 8, p], pl.ds(pl.multiple_of(m * ra, ra), ra), :]

    for k in range(nz):
        for p in range(npair):
            sx[k, p] = picked(far[k] * 2 + 1 - c, p)
        copy = remote(sx.at[k], rx.at[k], x_send.at[k], x_recv.at[k], {"ao": sib})
        copy.start()
        sent.append(copy)
    for k in range(nz):
        arrived(rx.at[k], x_recv.at[k])
        for p in range(npair):
            value = picked(far[k] * 2 + c, p) + rx[k, p]
            if k == here:
                own[p] = value
            else:
                ks[k, p] = value.astype(jnp.bfloat16)
        if k != here:
            copy = remote(ks.at[k], kr.at[z], k_send.at[k], k_recv.at[z], {"ao": far[k] * 2 + c})
            copy.start()
            sent.append(copy)
    total = own[...]
    for k in others:
        arrived(kr.at[far[k]], k_recv.at[far[k]])
        total += kr[far[k]].astype(jnp.float32)
    out[...] = total

    for copy in sent:
        copy.wait_send()

    def left_over(n, _):
        for j in range(npz):
            for d in range(1, nx):
                remote(
                    hbuf.at[x, j, n], hbuf.at[x, j, n], f_send.at[d, j, n], f_recv.at[x, j, n],
                    {"aux": (x + d) % nx},
                ).wait_send()
        return 0

    lax.fori_loop(0, nao, left_over, 0)


def per_device(nao, nx, three_index, orbitals, partners):
    npair, npl, blk, _ = three_index.shape
    wide = orbitals.shape[1]
    nz = nao // 2
    npz = npl // nz
    ra = blk // nx
    hw = wide // 2
    bf, f32 = jnp.bfloat16, jnp.float32
    dma = pltpu.SemaphoreType.DMA
    return pl.pallas_call(
        functools.partial(body, nao, nx),
        out_shape=jax.ShapeDtypeStruct((npair, ra, blk), f32),
        in_specs=[
            pl.BlockSpec(memory_space=pl.ANY),
            pl.BlockSpec(memory_space=pl.ANY),
            pl.BlockSpec(memory_space=pltpu.SMEM),
        ],
        out_specs=pl.BlockSpec(memory_space=pltpu.VMEM),
        scratch_shapes=[
            pltpu.VMEM((npair, npl, blk, blk), bf),
            pltpu.VMEM((nao, blk, wide), bf),
            pltpu.VMEM((npair * blk, wide), bf),
            pltpu.VMEM((nao * 8, 128), jnp.int32),
            pltpu.SMEM((nao * 8, 128), jnp.int32),
            pltpu.VMEM((npl, 2, blk, hw), bf),
            pltpu.VMEM((nx, npz, nao, blk, hw), bf),
            pltpu.VMEM((nao, nao * ra, blk), f32),
            pltpu.VMEM((nz, npair, ra, blk), f32),
            pltpu.VMEM((nz, npair, ra, blk), f32),
            pltpu.VMEM((nz, npair, ra, blk), bf),
            pltpu.VMEM((nz, npair, ra, blk), bf),
            pltpu.VMEM((npair, ra, blk), f32),
            dma((npair,)), dma, dma((nz,)), dma((nz,)), dma((nao,)),
            dma((nao,)), dma((nao,)), dma,
            dma((npl, 2)), dma((npz, nao)), dma((nx, npz, nao)), dma((nx, npz, nao)),
            dma((nz,)), dma((nz,)), dma((nz,)), dma((nz,)),
        ],
        compiler_params=pltpu.CompilerParams(
            collective_id=0, has_side_effects=True, vmem_limit_bytes=56 * 1024 * 1024,
        ),
    )(three_index, orbitals, partners)


def solution(mesh):
    placed = (P(("groups", "ao"), "aux", None, None), P("ao", "groups"), P(("groups", "ao"), None))
    return jax.shard_map(
        functools.partial(per_device, mesh.shape["ao"], mesh.shape["aux"]),
        mesh=mesh,
        in_specs=placed,
        out_specs=P(("groups", "ao"), "aux", None),
        check_vma=False,
    )
```

```python
import functools

import jax
import jax.numpy as jnp
from jax import lax
from jax.experimental import pallas as pl
from jax.experimental.pallas import tpu as pltpu
from jax.sharding import PartitionSpec as P

MESH = pl.DeviceIdType.MESH


def c_order(nz):
    return range(nz - 1, 0, -1)


def plan(npz, nz):
    out = list(dict.fromkeys([nz - 1, *range(1, nz - 1), 0]))
    back = list(dict.fromkeys([1, nz - 1, *range(2, nz - 1), 0]))
    steps = [("send", j, k) for j in range(npz) for k in out] + [("rows", 0, 0)]
    for j in range(npz):
        steps += [("pass", j, k) for k in back] + [("ship", j, 0)]
        if j > 0:
            steps += [("others", j - 1, 0)]
    return steps + [("lists", 0, 0), ("others", npz - 1, 0)]


def body(
    nao, nx,
    b_hbm, c_hbm, part, out,
    b_v, c_all, csel, pall, psm, hs, hsx, b_x, hbuf, kf, sx, rx, ks, kr, own,
    b_sem, c_loc, c_send, c_recv, s_send, s_recv, p_send, p_recv, p_loc,
    bx_send, bx_recv, h_send, h_recv, f_send, f_recv, x_send, x_recv, k_send, k_recv,
):
    me = lax.axis_index("ao")
    x = lax.axis_index("aux")
    nz = nao // 2
    z, c = me // 2, me % 2
    sib = z * 2 + 1 - c
    npair, npl, blk, _ = b_hbm.shape
    npz = npl // nz
    ra = blk // nx
    wide = c_hbm.shape[1]
    hw = wide // 2
    cuts = 2
    cr = blk // cuts

    def remote(src, dst, send, recv, where):
        return pltpu.make_async_remote_copy(
            src_ref=src, dst_ref=dst, send_sem=send, recv_sem=recv,
            device_id=where, device_id_type=MESH,
        )

    def arrived(ref, sem):
        remote(ref, ref, sem, sem, {"ao": sib}).wait_recv()

    def left(ref, sem):
        remote(ref, ref, sem, sem, {"ao": sib}).wait_send()

    met = []
    for k in range(nz):
        zk = z
        bit = 1
        while bit < nz:
            if k & bit:
                zk = zk + bit - 2 * bit * ((zk // bit) % 2)
            bit *= 2
        met.append(zk)

    mine = pltpu.make_async_copy(c_hbm, c_all.at[me], c_loc)
    mine.start()
    load = pltpu.make_async_copy(b_hbm, b_v, b_sem)
    load.start()

    barrier = pltpu.get_barrier_semaphore()
    pl.semaphore_signal(barrier, inc=1, device_id={"ao": sib}, device_id_type=MESH)
    for k in range(1, nx):
        pl.semaphore_signal(barrier, inc=1, device_id={"aux": (x + k) % nx}, device_id_type=MESH)

    for k in range(1, nz):
        pl.semaphore_signal(barrier, inc=1, device_id={"ao": met[k] * 2 + c}, device_id_type=MESH)
    pl.semaphore_wait(barrier, nx + nz - 1)

    for k in c_order(nz):
        for h in range(cuts):
            piece = pl.ds(h * cr, cr)
            remote(
                c_hbm.at[piece], c_all.at[me, piece], c_send, c_recv.at[k, h], {"ao": met[k] * 2 + c},
            ).start()
    remote(c_hbm, c_all.at[me], s_send, s_recv, {"ao": sib}).start()

    for d in range(1, nx):
        for p in range(npair):
            remote(
                b_hbm.at[p, pl.ds(z * npz, npz)], b_x.at[x, p], bx_send, bx_recv.at[x], {"aux": (x + d) % nx},
            ).start()

    for k in range(1, nz):
        for h in range(cuts):
            piece = c_all.at[met[k] * 2 + c, pl.ds(h * cr, cr)]
            arrived(piece, c_recv.at[k, h])
            remote(piece, piece, s_send, s_recv, {"ao": sib}).start()

    lane = lax.broadcasted_iota(jnp.int32, (8, 128), 1)
    row = jnp.zeros((8, 128), jnp.int32)
    for p in range(npair):
        row = jnp.where(lane == p, part[0, p], row)
    myrow = pall.at[pl.ds(pl.multiple_of(me * 8, 8), 8)]
    myrow[...] = row
    mine.wait()
    load.wait()
    arrived(c_all.at[pl.ds(0, nz)], s_recv)
    for p in range(npair):
        csel[p * blk:(p + 1) * blk, :] = c_all[part[0, p]]

    def pass_on(j, n, count):
        for d in range(1, nx):
            for i in range(count):
                piece = hbuf.at[x, j, n + i]
                remote(piece, piece, f_send.at[d], f_recv.at[x, j], {"aux": (x + d) % nx}).start()

    def transformed(blocks):
        rows = jnp.concatenate(blocks, axis=1)
        return jnp.dot(rows, csel[...], preferred_element_type=jnp.float32).astype(jnp.bfloat16)

    def send(j, k):
        q = met[k] * npz + j
        half = transformed([b_v[p, q] for p in range(npair)])
        hs[q, 0] = half[:, :hw]
        hs[q, 1] = half[:, hw:]
        if k == 0:
            hbuf[x, j, me] = hs[q, c]
            remote(hs.at[q, 1 - c], hbuf.at[x, j, me], h_send.at[1], h_recv.at[j, 0], {"ao": sib}).start()
        else:
            for cc in range(2):
                remote(
                    hs.at[q, cc], hbuf.at[x, j, me], h_send.at[0], h_recv.at[j, k], {"ao": met[k] * 2 + cc},
                ).start()


    def ship(j):
        for d in range(1, nx):
            xs = (x + d) % nx
            if j == 0:
                arrived(b_x.at[xs], bx_recv.at[xs])
            half = transformed([b_x[xs, p, j] for p in range(npair)])
            hsx[d, j, 0] = half[:, :hw]
            hsx[d, j, 1] = half[:, hw:]
            hbuf[xs, j, me] = hsx[d, j, c]
            remote(hsx.at[d, j, 1 - c], hbuf.at[xs, j, me], h_send.at[2], f_recv.at[xs, j], {"ao": sib}).start()

    def receive(j, k):
        if k == 0:
            arrived(hbuf.at[x, j, sib], h_recv.at[j, 0])
        else:
            arrived(hbuf.at[x, j, pl.ds(met[k] * 2, 2)], h_recv.at[j, k])
            pass_on(j, met[k] * 2, 2)

    def add_up(xs, j, first):
        lhs = hbuf[xs, j, :, pl.ds(pl.multiple_of(x * ra, ra), ra), :].reshape(nao * ra, hw)

        def step(t, _):
            rhs = hbuf[xs, j, pl.ds(2 * t, 2)].reshape(2 * blk, hw)
            got = lax.dot_general(lhs, rhs, (((1,), (1,)), ((), ())), preferred_element_type=jnp.float32)
            if first:
                kf[2 * t] = got[:, :blk]
                kf[2 * t + 1] = got[:, blk:]
            else:
                kf[2 * t] += got[:, :blk]
                kf[2 * t + 1] += got[:, blk:]
            return 0

        lax.fori_loop(0, nao // 2, step, 0)

    def take_others(j):
        for d in range(1, nx):
            xs = (x + d) % nx
            arrived(hbuf.at[xs, j, pl.ds(0, nao - 1)], f_recv.at[xs, j])
            add_up(xs, j, False)

    missing = [nz] * npz
    for kind, j, k in plan(npz, nz):
        if kind == "send":
            send(j, k)
        elif kind == "rows":
            for i in range(1, nao):
                remote(myrow, myrow, p_send, p_recv, {"ao": (me + i) % nao}).start()
        elif kind == "ship":
            ship(j)
        elif kind == "lists":
            arrived(pall.at[pl.ds(0, (nao - 1) * 8)], p_recv)
            to_smem = pltpu.make_async_copy(pall, psm, p_loc)
            to_smem.start()
            to_smem.wait()
        elif kind == "others":
            take_others(j)
        else:
            receive(j, k)
            missing[j] -= 1
            if missing[j] == 0:
                add_up(x, j, j == 0)


    def picked(m, p):
        return kf[psm[m * 8, p], pl.ds(pl.multiple_of(m * ra, ra), ra), :]

    for k in range(nz - 1, -1, -1):
        for p in range(npair):
            sx[k, p] = picked(met[k] * 2 + 1 - c, p)
        remote(sx.at[k], rx.at[k], x_send, x_recv.at[k], {"ao": sib}).start()
    for k in range(nz - 1, -1, -1):
        arrived(rx.at[k], x_recv.at[k])
        for p in range(npair):
            value = picked(met[k] * 2 + c, p) + rx[k, p]
            if k == 0:
                own[p] = value
            else:
                ks[k, p] = value.astype(jnp.bfloat16)
        if k > 0:
            remote(ks.at[k], kr.at[k], k_send, k_recv, {"ao": met[k] * 2 + c}).start()
    total = own[...]
    arrived(kr.at[pl.ds(1, nz - 1)], k_recv)
    for k in range(1, nz):
        total += kr[k].astype(jnp.float32)
    out[...] = total

    left(c_all.at[pl.ds(0, nz - 1)], c_send)
    left(c_all.at[pl.ds(0, nz)], s_send)
    left(pall.at[pl.ds(0, (nao - 1) * 8)], p_send)
    left(hs.at[pl.ds(0, npl - npz)], h_send.at[0])
    left(hs.at[pl.ds(0, npz), 0], h_send.at[1])
    left(hsx.at[pl.ds(1, nx - 1), :, 0], h_send.at[2])
    left(b_x.at[pl.ds(0, nx - 1)], bx_send)
    for d in range(1, nx):
        left(hbuf.at[x, :, pl.ds(0, nao - 2)], f_send.at[d])
    left(rx, x_send)
    left(ks.at[pl.ds(1, nz - 1)], k_send)


def per_device(nao, nx, three_index, orbitals, partners):
    npair, npl, blk, _ = three_index.shape
    wide = orbitals.shape[1]
    nz = nao // 2
    npz = npl // nz
    ra = blk // nx
    hw = wide // 2
    bf, f32 = jnp.bfloat16, jnp.float32
    dma = pltpu.SemaphoreType.DMA
    return pl.pallas_call(
        functools.partial(body, nao, nx),
        out_shape=jax.ShapeDtypeStruct((npair, ra, blk), f32),
        in_specs=[
            pl.BlockSpec(memory_space=pl.ANY),
            pl.BlockSpec(memory_space=pl.ANY),
            pl.BlockSpec(memory_space=pltpu.SMEM),
        ],
        out_specs=pl.BlockSpec(memory_space=pltpu.VMEM),
        scratch_shapes=[
            pltpu.VMEM((npair, npl, blk, blk), bf),
            pltpu.VMEM((nao, blk, wide), bf),
            pltpu.VMEM((npair * blk, wide), bf),
            pltpu.VMEM((nao * 8, 128), jnp.int32),
            pltpu.SMEM((nao * 8, 128), jnp.int32),
            pltpu.VMEM((npl, 2, blk, hw), bf),
            pltpu.VMEM((nx, npz, 2, blk, hw), bf),
            pltpu.VMEM((nx, npair, npz, blk, blk), bf),
            pltpu.VMEM((nx, npz, nao, blk, hw), bf),
            pltpu.VMEM((nao, nao * ra, blk), f32),
            pltpu.VMEM((nz, npair, ra, blk), f32),
            pltpu.VMEM((nz, npair, ra, blk), f32),
            pltpu.VMEM((nz, npair, ra, blk), bf),
            pltpu.VMEM((nz, npair, ra, blk), bf),
            pltpu.VMEM((npair, ra, blk), f32),
            dma, dma, dma, dma((nz, 2)), dma, dma, dma, dma, dma,
            dma, dma((nx,)), dma((3,)), dma((npz, nz)), dma((nx,)), dma((nx, npz)),
            dma, dma((nz,)), dma, dma,
        ],
        compiler_params=pltpu.CompilerParams(
            collective_id=0, has_side_effects=True, vmem_limit_bytes=56 * 1024 * 1024,
        ),
    )(three_index, orbitals, partners)


def solution(mesh):
    placed = (P(("groups", "ao"), "aux", None, None), P("ao", "groups"), P(("groups", "ao"), None))
    return jax.shard_map(
        functools.partial(per_device, mesh.shape["ao"], mesh.shape["aux"]),
        mesh=mesh,
        in_specs=placed,
        out_specs=P(("groups", "ao"), "aux", None),
        check_vma=False,
    )
```

```python
import functools

import jax
import jax.numpy as jnp
from jax import lax
from jax.experimental import pallas as pl
from jax.experimental.pallas import tpu as pltpu
from jax.sharding import PartitionSpec as P

MESH = pl.DeviceIdType.MESH


def c_order(nz):
    return range(nz - 1, 0, -1)


def plan(npz, nz):
    out = list(dict.fromkeys([nz - 1, *range(1, nz - 1), 0]))
    back = list(dict.fromkeys([1, nz - 1, *range(2, nz - 1), 0]))
    steps = [("send", j, k) for j in range(npz) for k in out] + [("rows", 0, 0)]
    for j in range(npz):
        steps += [("pass", j, k) for k in back] + [("ship", j, 0)]
        if j > 0:
            steps += [("others", j - 1, 0)]
    return steps + [("lists", 0, 0), ("others", npz - 1, 0)]


def body(
    nao, nx,
    b_hbm, c_hbm, part, own, rest,
    b_v, c_all, csel, pall, psm, hs, hsx, b_x, hbuf, kf, sx, rx, ks, kr,
    b_sem, c_loc, c_send, c_recv, s_send, s_recv, p_send, p_recv, p_loc,
    bx_send, bx_recv, h_send, h_recv, f_send, f_recv, x_send, x_recv, k_send, k_recv,
):
    me = lax.axis_index("ao")
    x = lax.axis_index("aux")
    nz = nao // 2
    z, c = me // 2, me % 2
    sib = z * 2 + 1 - c
    npair, npl, blk, _ = b_hbm.shape
    npz = npl // nz
    ra = blk // nx
    wide = c_hbm.shape[1]
    hw = wide // 2
    cuts = 2
    cr = blk // cuts

    def remote(src, dst, send, recv, where):
        return pltpu.make_async_remote_copy(
            src_ref=src, dst_ref=dst, send_sem=send, recv_sem=recv,
            device_id=where, device_id_type=MESH,
        )

    def arrived(ref, sem):
        remote(ref, ref, sem, sem, {"ao": sib}).wait_recv()

    def left(ref, sem):
        remote(ref, ref, sem, sem, {"ao": sib}).wait_send()

    met = []
    for k in range(nz):
        zk = z
        bit = 1
        while bit < nz:
            if k & bit:
                zk = zk + bit - 2 * bit * ((zk // bit) % 2)
            bit *= 2
        met.append(zk)

    mine = pltpu.make_async_copy(c_hbm, c_all.at[me], c_loc)
    mine.start()
    load = pltpu.make_async_copy(b_hbm, b_v, b_sem)
    load.start()

    barrier = pltpu.get_barrier_semaphore()
    pl.semaphore_signal(barrier, inc=1, device_id={"ao": sib}, device_id_type=MESH)
    for k in range(1, nx):
        pl.semaphore_signal(barrier, inc=1, device_id={"aux": (x + k) % nx}, device_id_type=MESH)

    for k in range(1, nz):
        pl.semaphore_signal(barrier, inc=1, device_id={"ao": met[k] * 2 + c}, device_id_type=MESH)
    pl.semaphore_wait(barrier, nx + nz - 1)

    for k in c_order(nz):
        for h in range(cuts):
            piece = pl.ds(h * cr, cr)
            remote(
                c_hbm.at[piece], c_all.at[me, piece], c_send, c_recv.at[k, h], {"ao": met[k] * 2 + c},
            ).start()
    remote(c_hbm, c_all.at[me], s_send, s_recv, {"ao": sib}).start()

    for d in range(1, nx):
        for p in range(npair):
            remote(
                b_hbm.at[p, pl.ds(z * npz, npz)], b_x.at[x, p], bx_send, bx_recv.at[x], {"aux": (x + d) % nx},
            ).start()

    for k in range(1, nz):
        for h in range(cuts):
            piece = c_all.at[met[k] * 2 + c, pl.ds(h * cr, cr)]
            arrived(piece, c_recv.at[k, h])
            remote(piece, piece, s_send, s_recv, {"ao": sib}).start()

    lane = lax.broadcasted_iota(jnp.int32, (8, 128), 1)
    row = jnp.zeros((8, 128), jnp.int32)
    for p in range(npair):
        row = jnp.where(lane == p, part[0, p], row)
    myrow = pall.at[pl.ds(pl.multiple_of(me * 8, 8), 8)]
    myrow[...] = row
    mine.wait()
    load.wait()
    arrived(c_all.at[pl.ds(0, nz)], s_recv)
    for p in range(npair):
        csel[p * blk:(p + 1) * blk, :] = c_all[part[0, p]]

    def pass_on(j, n, count):
        for d in range(1, nx):
            for i in range(count):
                piece = hbuf.at[x, j, n + i]
                remote(piece, piece, f_send.at[d], f_recv.at[x, j], {"aux": (x + d) % nx}).start()

    def transformed(blocks):
        rows = jnp.concatenate(blocks, axis=1)
        return jnp.dot(rows, csel[...], preferred_element_type=jnp.float32).astype(jnp.bfloat16)

    def send(j, k):
        q = met[k] * npz + j
        half = transformed([b_v[p, q] for p in range(npair)])
        hs[q, 0] = half[:, :hw]
        hs[q, 1] = half[:, hw:]
        if k == 0:
            hbuf[x, j, me] = hs[q, c]
            remote(hs.at[q, 1 - c], hbuf.at[x, j, me], h_send.at[1], h_recv.at[j, 0], {"ao": sib}).start()
        else:
            for cc in range(2):
                remote(
                    hs.at[q, cc], hbuf.at[x, j, me], h_send.at[0], h_recv.at[j, k], {"ao": met[k] * 2 + cc},
                ).start()


    def ship(j):
        for d in range(1, nx):
            xs = (x + d) % nx
            if j == 0:
                arrived(b_x.at[xs], bx_recv.at[xs])
            half = transformed([b_x[xs, p, j] for p in range(npair)])
            hsx[d, j, 0] = half[:, :hw]
            hsx[d, j, 1] = half[:, hw:]
            hbuf[xs, j, me] = hsx[d, j, c]
            remote(hsx.at[d, j, 1 - c], hbuf.at[xs, j, me], h_send.at[2], f_recv.at[xs, j], {"ao": sib}).start()

    def receive(j, k):
        if k == 0:
            arrived(hbuf.at[x, j, sib], h_recv.at[j, 0])
        else:
            arrived(hbuf.at[x, j, pl.ds(met[k] * 2, 2)], h_recv.at[j, k])
            pass_on(j, met[k] * 2, 2)

    def add_up(xs, j, first):
        lhs = hbuf[xs, j, :, pl.ds(pl.multiple_of(x * ra, ra), ra), :].reshape(nao * ra, hw)

        def step(t, _):
            rhs = hbuf[xs, j, pl.ds(2 * t, 2)].reshape(2 * blk, hw)
            got = lax.dot_general(lhs, rhs, (((1,), (1,)), ((), ())), preferred_element_type=jnp.float32)
            if first:
                kf[2 * t] = got[:, :blk]
                kf[2 * t + 1] = got[:, blk:]
            else:
                kf[2 * t] += got[:, :blk]
                kf[2 * t + 1] += got[:, blk:]
            return 0

        lax.fori_loop(0, nao // 2, step, 0)

    def take_others(j):
        for d in range(1, nx):
            xs = (x + d) % nx
            arrived(hbuf.at[xs, j, pl.ds(0, nao - 1)], f_recv.at[xs, j])
            add_up(xs, j, False)

    missing = [nz] * npz
    for kind, j, k in plan(npz, nz):
        if kind == "send":
            send(j, k)
        elif kind == "rows":
            for i in range(1, nao):
                remote(myrow, myrow, p_send, p_recv, {"ao": (me + i) % nao}).start()
        elif kind == "ship":
            ship(j)
        elif kind == "lists":
            arrived(pall.at[pl.ds(0, (nao - 1) * 8)], p_recv)
            to_smem = pltpu.make_async_copy(pall, psm, p_loc)
            to_smem.start()
            to_smem.wait()
        elif kind == "others":
            take_others(j)
        else:
            receive(j, k)
            missing[j] -= 1
            if missing[j] == 0:
                add_up(x, j, j == 0)


    def picked(m, p):
        return kf[psm[m * 8, p], pl.ds(pl.multiple_of(m * ra, ra), ra), :]

    for k in range(nz - 1, -1, -1):
        for p in range(npair):
            sx[k, p] = picked(met[k] * 2 + 1 - c, p)
        remote(sx.at[k], rx.at[k], x_send, x_recv.at[k], {"ao": sib}).start()
    for k in range(nz - 1, -1, -1):
        arrived(rx.at[k], x_recv.at[k])
        for p in range(npair):
            value = picked(met[k] * 2 + c, p) + rx[k, p]
            if k == 0:
                own[p] = value
            else:
                ks[k, p] = value.astype(jnp.bfloat16)
        if k > 0:
            remote(ks.at[k], kr.at[k], k_send, k_recv, {"ao": met[k] * 2 + c}).start()
    arrived(kr.at[pl.ds(1, nz - 1)], k_recv)
    total = kr[1].astype(jnp.float32)
    for k in range(2, nz):
        total += kr[k].astype(jnp.float32)
    rest[...] = total

    left(c_all.at[pl.ds(0, nz - 1)], c_send)
    left(c_all.at[pl.ds(0, nz)], s_send)
    left(pall.at[pl.ds(0, (nao - 1) * 8)], p_send)
    left(hs.at[pl.ds(0, npl - npz)], h_send.at[0])
    left(hs.at[pl.ds(0, npz), 0], h_send.at[1])
    left(hsx.at[pl.ds(1, nx - 1), :, 0], h_send.at[2])
    left(b_x.at[pl.ds(0, nx - 1)], bx_send)
    for d in range(1, nx):
        left(hbuf.at[x, :, pl.ds(0, nao - 2)], f_send.at[d])
    left(rx, x_send)
    left(ks.at[pl.ds(1, nz - 1)], k_send)


def per_device(nao, nx, three_index, orbitals, partners):
    npair, npl, blk, _ = three_index.shape
    wide = orbitals.shape[1]
    nz = nao // 2
    npz = npl // nz
    ra = blk // nx
    hw = wide // 2
    bf, f32 = jnp.bfloat16, jnp.float32
    dma = pltpu.SemaphoreType.DMA
    own, rest = pl.pallas_call(
        functools.partial(body, nao, nx),
        out_shape=[jax.ShapeDtypeStruct((npair, ra, blk), f32)] * 2,
        in_specs=[
            pl.BlockSpec(memory_space=pl.ANY),
            pl.BlockSpec(memory_space=pl.ANY),
            pl.BlockSpec(memory_space=pltpu.SMEM),
        ],
        out_specs=[pl.BlockSpec(memory_space=pltpu.VMEM)] * 2,
        scratch_shapes=[
            pltpu.VMEM((npair, npl, blk, blk), bf),
            pltpu.VMEM((nao, blk, wide), bf),
            pltpu.VMEM((npair * blk, wide), bf),
            pltpu.VMEM((nao * 8, 128), jnp.int32),
            pltpu.SMEM((nao * 8, 128), jnp.int32),
            pltpu.VMEM((npl, 2, blk, hw), bf),
            pltpu.VMEM((nx, npz, 2, blk, hw), bf),
            pltpu.VMEM((nx, npair, npz, blk, blk), bf),
            pltpu.VMEM((nx, npz, nao, blk, hw), bf),
            pltpu.VMEM((nao, nao * ra, blk), f32),
            pltpu.VMEM((nz, npair, ra, blk), f32),
            pltpu.VMEM((nz, npair, ra, blk), f32),
            pltpu.VMEM((nz, npair, ra, blk), bf),
            pltpu.VMEM((nz, npair, ra, blk), bf),
            dma, dma, dma, dma((nz, 2)), dma, dma, dma, dma, dma,
            dma, dma((nx,)), dma((3,)), dma((npz, nz)), dma((nx,)), dma((nx, npz)),
            dma, dma((nz,)), dma, dma,
        ],
        compiler_params=pltpu.CompilerParams(
            collective_id=0, has_side_effects=True, vmem_limit_bytes=56 * 1024 * 1024,
        ),
    )(three_index, orbitals, partners)
    return own + rest


def solution(mesh):
    placed = (P(("groups", "ao"), "aux", None, None), P("ao", "groups"), P(("groups", "ao"), None))
    return jax.shard_map(
        functools.partial(per_device, mesh.shape["ao"], mesh.shape["aux"]),
        mesh=mesh,
        in_specs=placed,
        out_specs=P(("groups", "ao"), "aux", None),
        check_vma=False,
    )
```
